256 devices in a mesh: rep: 32 (over z_hi, y, x), inner: 8 (over z_lo, core).
Axes of the slice: x: 4, y: 4, z: 8 (z_hi: 2, z_lo: 4; z = z_hi * 4 + z_lo), core: 2. Of those that a mesh axis runs over, the one named last changes fastest.
Arguments:
- deltas: bfloat16 [32, 5120, 2560], P('rep', 'inner'), may hold values from -6 to 6
- master_weight: float32 [5120, 2560], P(('inner', 'rep')), may hold values from -6 to 6
- momentum: float32 [5120, 2560], P(('inner', 'rep')), may hold values from -4 to 4
Outputs:
- weights_out: bfloat16 [5120, 2560], P('inner')
- master_out: float32 [5120, 2560], P(('inner', 'rep'))
- momentum_out: float32 [5120, 2560], P(('inner', 'rep'))
The draws below stay inside these ranges and needn't reach their ends.
All inputs are finite; a program needn't handle non-finite values.
Results may differ from the reference program's by a relative error of at most 0.014.
Values may be sent and summed in bfloat16 or wider, within the bound.
No kernel may reach another device: no remote copies, remote signals or barrier semaphores. Data moves between devices by JAX's collectives and lax.ppermute only.
A program may use at most 64 MiB of HBM per device.

```python
import jax
import jax.numpy as jnp
from jax import lax

D = 2560
FF_IN = 5120
N_REP = 32


def spiked(drawn, own_key, source, target, shards_of, factor):
    owner, partner = [(jnp.arange(drawn.shape[axis_at]) // (drawn.shape[axis_at] // shards_of)).reshape([-1 if axis == axis_at else 1 for axis in range(drawn.ndim)]) for axis_at in (source, target)]
    chosen = jax.random.permutation(own_key, shards_of)[partner]
    strong = (owner == chosen) | (owner == (partner + shards_of // 2) % shards_of)
    return jnp.where(strong, factor * drawn, drawn)


def shard_levels(stream_key, dims, pieces, least, high):
    def one(position, parts):
        heights = jax.random.uniform(jax.random.fold_in(jax.random.fold_in(stream_key, 6), position), (parts,), jnp.float32, least / len(pieces), high / len(pieces))
        return jnp.repeat(jnp.exp(heights), dims[position] // parts).reshape((-1,) + (1,) * (len(dims) - position - 1))

    level = one(*pieces[0])
    for cut in pieces[1:]:
        level = level * one(*cut)
    return level


def bell_draw(stream_key, extent, scale, limit, split=(), dtype=jnp.bfloat16):
    factor_of = shard_levels(stream_key, extent, split, -0.22, 0.18) if split else 1.0
    values = jax.random.normal(stream_key, extent, jnp.float32) * scale * factor_of
    return jnp.minimum(jnp.maximum(values, -limit), limit).astype(dtype)


def heavy_noise(own_key, shape, spread, limit, split, heavy, held_as=jnp.bfloat16):
    result = spread * jax.random.normal(own_key, shape, jnp.float32)
    if split:
        result = result * shard_levels(own_key, shape, split, -0.22, 0.18)
    return jnp.clip(spiked(result, jax.random.fold_in(own_key, 3), *heavy), -limit, limit).astype(held_as)


def setup_inputs(seed: int = 0) -> dict:
    arg_keys = jax.random.split(jax.random.key(seed), 4)
    return {
        "deltas": heavy_noise(arg_keys[0], (N_REP, FF_IN, D), 1.0, 6.0, ((0, 32), (1, 8)), (0, 1, 32, 2.75)),
        "master_weight": bell_draw(arg_keys[1], (FF_IN, D), 1.0, 6.0, ((0, 256),), jnp.float32),
        "momentum": bell_draw(arg_keys[2], (FF_IN, D), 0.3, 4.0, ((0, 256),), jnp.float32),
    }


outer_rate = 0.7
momentum_decay = 0.9


def reference(deltas, master_weight, momentum):
    def accumulate(index, running):
        return running + deltas[index].astype(jnp.float32)

    summed = lax.fori_loop(0, N_REP, accumulate, jnp.zeros(master_weight.shape, jnp.float32))
    average = summed / N_REP
    momentum_out = momentum_decay * momentum + average
    master_out = master_weight - outer_rate * (average + momentum_decay * momentum_out)
    weights_out = master_out.astype(jnp.bfloat16)
    return weights_out, master_out, momentum_out
```

```python
import jax
import jax.numpy as jnp
from jax import lax
from jax.experimental import pallas as pl
from jax.experimental.pallas import tpu as pltpu
from jax.sharding import Mesh, PartitionSpec as P

N_REP = 32
OUTER_RATE = 0.7
DECAY = 0.9
AXES = ("zhi", "y", "x", "inner")
SIZES = (2, 4, 4, 8)
D = 2560
HALF = D // 2
ROWS = 20
BLOCK = 80
F32 = jnp.float32
BF16 = jnp.bfloat16


def shift_pairs(axis, step):
    at = AXES.index(axis)
    stride = 1
    for size in SIZES[at + 1:]:
        stride *= size
    total = 256
    pairs = []
    for device in range(total):
        place = device // stride % SIZES[at]
        pairs.append((device, device + ((place + step) % SIZES[at] - place) * stride))
    return pairs


def shifted(array, axis, step):
    return lax.ppermute(array, AXES, shift_pairs(axis, step))


def call(body, outs, *args, scratch=()):
    moved = sum(a.size * a.dtype.itemsize for a in (*args, *outs))
    return pl.pallas_call(
        body,
        out_shape=outs,
        in_specs=[pl.BlockSpec(memory_space=pltpu.VMEM)] * len(args),
        out_specs=[pl.BlockSpec(memory_space=pltpu.VMEM)] * len(outs),
        scratch_shapes=scratch,
        cost_estimate=pl.CostEstimate(flops=moved, bytes_accessed=moved, transcendentals=0),
        compiler_params=pltpu.CompilerParams(vmem_limit_bytes=40 * 2**20),
    )(*args)


def like(shape, dtype):
    return jax.ShapeDtypeStruct(shape, dtype)


def pack(d_ref, *out):
    x, y = lax.axis_index("x"), lax.axis_index("y")
    for s in range(4):
        for j in range(4):
            @pl.when(lax.rem(x + s, 4) == j)
            def _():
                for k in range(4):
                    out[s][pl.ds(ROWS * k, ROWS), :] = d_ref[k, pl.ds(ROWS * j, ROWS), :]
        out[4 + s][...] = d_ref[4 + lax.rem(y + s, 4)]


def narrow(value):
    return jnp.concatenate([value[:, :HALF], value[:, HALF:]], axis=0)


def wide(value):
    return jnp.concatenate([value[:ROWS], value[ROWS:]], axis=1)


def first_sum(*refs):
    parts, out, total = refs[:8], refs[8:16], refs[16]
    x, y = lax.axis_index("x"), lax.axis_index("y")
    for h, place in ((0, y), (1, x)):
        for k in range(4):
            rows = pl.ds(ROWS * k, ROWS)
            value = parts[4 * h][rows, :].astype(F32)
            for s in range(1, 4):
                value = value + parts[4 * h + s][rows, :].astype(F32)
            total[h, k] = value
        for s in range(4):
            value = total[h, lax.rem(place + s, 4)]
            o = out[4 * h + s]
            o[pl.ds(0, ROWS), :] = value[:, :HALF].astype(o.dtype)
            o[pl.ds(ROWS, ROWS), :] = value[:, HALF:].astype(o.dtype)


def second_sum(*refs):
    parts, out = refs[:8], refs[8]
    for h in range(2):
        value = parts[4 * h][...]
        for s in range(1, 4):
            value = value + parts[4 * h + s][...].astype(F32)
        out[h] = value.astype(BF16)


def update(own, other, base_own, base_other, momentum, weights, master_out, momentum_out):
    z = lax.axis_index("zhi")
    for h in range(2):
        average = (own[h].astype(F32) + other[h].astype(F32)) * (1.0 / N_REP)

        def halves(ref_base, row_average, col):
            return ref_base[:, col * HALF:(col + 1) * HALF] - (OUTER_RATE * (1 + DECAY)) * row_average

        for col in range(2):
            part = average[ROWS * col:ROWS * (col + 1)]
            cols = pl.ds(HALF * col, HALF)

            @pl.when(z == h)
            def _():
                momentum_out[:, cols] = DECAY * momentum[:, cols] + part
                new = base_own[:, cols] - (OUTER_RATE * (1 + DECAY)) * part
                master_out[:, cols] = new
                weights[h, pl.ds(ROWS * col, ROWS), :] = new.astype(BF16)

            @pl.when(z != h)
            def _():
                new = base_other[:, cols] - (OUTER_RATE * (1 + DECAY)) * part
                weights[h, pl.ds(ROWS * col, ROWS), :] = new.astype(BF16)


def join(weights, *refs):
    for h in range(2):
        out = refs[6 + h]
        out[0] = weights[h]
        for s in range(1, 4):
            out[s] = refs[3 * h + s - 1][...]


def unpack(*refs):
    parts, out = refs[:8], refs[8]
    x, y = lax.axis_index("x"), lax.axis_index("y")
    for s in range(4):
        for t in range(4):
            for j in range(4):
                @pl.when(lax.rem(x + 4 - t, 4) == j)
                def _():
                    row = lax.rem(y + 4 - s, 4)
                    for col in range(2):
                        out[row, pl.ds(ROWS * j, ROWS), pl.ds(HALF * col, HALF)] = parts[t][s, pl.ds(ROWS * col, ROWS), :]
                    row = 4 + lax.rem(y + 4 - s, 4)
                    for col in range(2):
                        out[row, pl.ds(ROWS * j, ROWS), pl.ds(HALF * col, HALF)] = parts[4 + s][t, pl.ds(ROWS * col, ROWS), :]


def local(deltas, master, momentum):
    d = deltas.reshape(8, BLOCK, D)
    packed = call(pack, [like((BLOCK, D), BF16)] * 8, d)
    a, b = list(packed[:4]), list(packed[4:])
    for s in (1, 3, 2):
        a[s] = shifted(packed[s], "x", s)
        b[s] = shifted(packed[4 + s], "y", s)
    base = master - (OUTER_RATE * DECAY * DECAY) * momentum
    base_other = shifted(base, "zhi", 1)

    small = (2 * ROWS, HALF)
    firsts = call(
        first_sum, ([like(small, F32)] + [like(small, BF16)] * 3) * 2, *a, *b,
        scratch=[pltpu.VMEM((2, 4, ROWS, D), F32)],
    )
    a, b = list(firsts[:4]), list(firsts[4:])
    for s in (1, 3, 2):
        a[s] = shifted(firsts[s], "y", s)
        b[s] = shifted(firsts[4 + s], "x", s)
    (own,) = call(second_sum, [like((2,) + small, BF16)], *a, *b)
    other = shifted(own, "zhi", 1)
    weights, master_out, momentum_out = call(
        update, [like((2,) + small, BF16), like((ROWS, D), F32), like((ROWS, D), F32)],
        own, other, base, base_other, momentum,
    )
    a = [shifted(weights[0], "y", s) for s in range(1, 4)]
    b = [shifted(weights[1], "x", s) for s in range(1, 4)]
    joined = call(join, [like((4,) + small, BF16)] * 2, weights, *a, *b)
    a = [joined[0]] + [shifted(joined[0], "x", s) for s in range(1, 4)]
    b = [joined[1]] + [shifted(joined[1], "y", s) for s in range(1, 4)]
    (out,) = call(unpack, [like((8, BLOCK, D), BF16)], *a, *b)
    return out.reshape(8 * BLOCK, D), master_out, momentum_out


def solution(mesh):
    parts = Mesh(mesh.devices.reshape(SIZES), AXES)
    rep = ("zhi", "y", "x")
    rows = P(("inner",) + rep, None)
    return jax.shard_map(
        local,
        mesh=parts,
        in_specs=(P(rep, "inner", None), rows, rows),
        out_specs=(P("inner", None), rows, rows),
        check_vma=False,
    )
```

```python
import functools

import jax
import jax.numpy as jnp
from jax import lax
from jax.experimental import pallas as pl
from jax.experimental.pallas import tpu as pltpu
from jax.sharding import Mesh, PartitionSpec as P

N_REP = 32
OUTER_RATE = 0.7
DECAY = 0.9
SCALE = OUTER_RATE * (1 + DECAY)
AXES = ("zhi", "y", "x", "inner")
SIZES = (2, 4, 4, 8)
D = 2560
HALF = D // 2
ROWS = 20
BLOCK = 80
SMALL = (2 * ROWS, HALF)
FOUR = (4,) + SMALL
F32 = jnp.float32
BF16 = jnp.bfloat16
ANY = pl.BlockSpec(memory_space=pl.ANY)
HBM = pl.BlockSpec(memory_space=pltpu.HBM)
VMEM = pl.BlockSpec(memory_space=pltpu.VMEM)
FIRST = (1, 3, 2)
MIDDLE = (1, 3, 2)
GATHER = (2, 3, 1)
LAST = (2, 3, 1)


def moved(array, axis, place):
    at = AXES.index(axis)
    stride = 1
    for size in SIZES[at + 1:]:
        stride *= size
    pairs = []
    for device in range(256):
        p = device // stride % SIZES[at]
        pairs.append((device, device + (place(p) - p) * stride))
    return lax.ppermute(array, AXES, pairs)


def shifted(array, axis, step):
    return moved(array, axis, lambda p: (p + step) % SIZES[AXES.index(axis)])


def swapped(array, axis, mask):
    return moved(array, axis, lambda p: p ^ mask)


def received(parts, axis, order):
    return [parts[0]] + [shifted(parts[s], axis, s) for s in order]


def call(body, outs, *args, scratch=(), aliases=None, specs=None, after=()):
    size = sum(a.size * a.dtype.itemsize for a in (*args, *outs))
    in_specs, out_specs = specs or ([VMEM] * len(args), [VMEM] * len(outs))
    count = len(args)
    args = (*args, *after)

    def kernel(*refs):
        body(*refs[:count], *refs[len(args):])

    return pl.pallas_call(
        kernel,
        out_shape=outs,
        in_specs=in_specs + [ANY] * len(after),
        out_specs=out_specs,
        scratch_shapes=scratch,
        input_output_aliases=aliases or {},
        cost_estimate=pl.CostEstimate(flops=size, bytes_accessed=size, transcendentals=0),
        compiler_params=pltpu.CompilerParams(vmem_limit_bytes=40 * 2**20),
    )(*args)


def like(shape, dtype):
    return jax.ShapeDtypeStruct(shape, dtype)


def pack_rows(d_ref, *out):
    x = lax.axis_index("x")
    for s in range(4):
        for j in range(4):
            @pl.when(lax.rem(x + s, 4) == j)
            def _():
                for k in range(4):
                    out[s][pl.ds(ROWS * k, ROWS), :] = d_ref[k, pl.ds(ROWS * j, ROWS), :]


def first_sum(axis, *refs):
    parts, out, total = refs[:4], refs[4:8], refs[8]
    place = lax.axis_index(axis)
    for k in range(4):
        rows = pl.ds(ROWS * k, ROWS)
        value = parts[0][rows, :].astype(F32)
        for s in range(1, 4):
            value = value + parts[s][rows, :].astype(F32)
        total[k] = value
    for s in range(4):
        value = total[lax.rem(place + s, 4)]
        o = out[s]
        for col in range(2):
            o[pl.ds(ROWS * col, ROWS), :] = value[:, HALF * col:HALF * (col + 1)].astype(o.dtype)


def second_sum(*refs):
    value = refs[0][...]
    for part in refs[1:4]:
        value = value + part[...].astype(F32)
    refs[4][...] = value.astype(BF16)


def early_base(master, momentum, base):
    base[...] = master[...] - (OUTER_RATE * DECAY * DECAY) * momentum[...]


def new_rows(owner, own, other, base_own, base_other, weights):
    mine = lax.axis_index("zhi") == owner
    for col in range(2):
        rows, cols = pl.ds(ROWS * col, ROWS), pl.ds(HALF * col, HALF)
        average = (own[rows, :].astype(F32) + other[rows, :].astype(F32)) * (1.0 / N_REP)
        base = jnp.where(mine, base_own[:, cols], base_other[:, cols])
        weights[rows, :] = (base - SCALE * average).astype(BF16)


def new_state(own_a, other_a, own_b, other_b, base, momentum, master_out, momentum_out):
    first = lax.axis_index("zhi") == 1
    for col in range(2):
        rows, cols = pl.ds(ROWS * col, ROWS), pl.ds(HALF * col, HALF)
        own = jnp.where(first, own_a[rows, :].astype(F32), own_b[rows, :].astype(F32))
        other = jnp.where(first, other_a[rows, :].astype(F32), other_b[rows, :].astype(F32))
        average = (own + other) * (1.0 / N_REP)
        momentum_out[:, cols] = DECAY * momentum[:, cols] + average
        master_out[:, cols] = base[:, cols] - SCALE * average


def join(*refs):
    for h in range(2):
        for part, s in enumerate((0,) + GATHER):
            refs[8 + h][s] = refs[4 * h + part][...]


def unpack_rows(*refs):
    parts, out, block, sems = refs[:4], refs[4], refs[5], refs[6]
    x, y = lax.axis_index("x"), lax.axis_index("y")
    copies = []
    for i in range(4):
        for part, t in enumerate((0,) + LAST):
            for j in range(4):
                @pl.when(lax.rem(x + 4 - t, 4) == j)
                def _():
                    for col in range(2):
                        block[i, pl.ds(ROWS * j, ROWS), pl.ds(HALF * col, HALF)] = parts[part][i, pl.ds(ROWS * col, ROWS), :]
        copies.append(pltpu.make_async_copy(block.at[i], out.at[lax.rem(y + 4 - i, 4)], sems.at[i]))
        copies[-1].start()
    for copy in copies:
        copy.wait()


def unpack_blocks(steps, *refs):
    count = len(steps)
    parts, out, block, sems = refs[:count], refs[count + 1], refs[count + 2], refs[count + 3]
    x, y = lax.axis_index("x"), lax.axis_index("y")
    copies = []
    for part, t in enumerate(steps):
        for i in range(4):
            for j in range(4):
                @pl.when(lax.rem(x + 4 - i, 4) == j)
                def _():
                    for col in range(2):
                        block[part, pl.ds(ROWS * j, ROWS), pl.ds(HALF * col, HALF)] = parts[part][i, pl.ds(ROWS * col, ROWS), :]
        copies.append(pltpu.make_async_copy(block.at[part], out.at[4 + lax.rem(y + 4 - t, 4)], sems.at[part]))
        copies[-1].start()
    for copy in copies:
        copy.wait()


def local(deltas, master, momentum):
    d = deltas.reshape(8, BLOCK, D)
    big = like((BLOCK, D), BF16)
    y = lax.axis_index("y")
    a = [lax.dynamic_index_in_dim(d, 4 + (y + s) % 4, keepdims=False) for s in range(4)]
    b = call(pack_rows, [big] * 4, d[:4])
    a = received(a, "y", FIRST)
    b = received(b, "x", FIRST)
    (base,) = call(early_base, [like((ROWS, D), F32)], master, momentum, after=[a[1]])
    base_other = swapped(base, "zhi", 1)

    outs = [like(SMALL, F32)] + [like(SMALL, BF16)] * 3
    total = [pltpu.VMEM((4, ROWS, D), F32)]
    sum_a = call(functools.partial(first_sum, "x"), outs, *a, scratch=total)
    sum_b = call(functools.partial(first_sum, "y"), outs, *b, scratch=total, after=[sum_a[0]])
    outs = [like(SMALL, BF16)]
    (own_a,) = call(second_sum, outs, *received(sum_a, "x", MIDDLE), after=[sum_b[0], base_other])
    (own_b,) = call(second_sum, outs, *received(sum_b, "y", MIDDLE), after=[own_a])
    other_a = swapped(own_a, "zhi", 1)
    other_b = swapped(own_b, "zhi", 1)
    (new_a,) = call(
        functools.partial(new_rows, 1), outs, own_a, other_a, base, base_other, after=[own_b],
    )
    (new_b,) = call(
        functools.partial(new_rows, 0), outs, own_b, other_b, base, base_other, after=[new_a],
    )
    all_a, all_b = call(
        join, [like(FOUR, BF16)] * 2,
        *received([new_a] * 4, "x", GATHER), *received([new_b] * 4, "y", GATHER),
    )
    master_out, momentum_out = call(
        new_state, [like((ROWS, D), F32)] * 2, own_a, other_a, own_b, other_b, base, momentum, after=[all_b],
    )
    a = received([all_a] * 4, "y", LAST)
    b = received([all_b] * 4, "x", LAST)
    whole = like((8, BLOCK, D), BF16)
    steps = (0,) + LAST

    def room(count):
        return [pltpu.VMEM((count, BLOCK, D), BF16), pltpu.SemaphoreType.DMA((count,))]

    (out,) = call(unpack_rows, [whole], *b, scratch=room(4), specs=([VMEM] * 4, [ANY]))
    for part in ((0, 1, 2), (3,)):
        n = len(part)
        (out,) = call(
            functools.partial(unpack_blocks, [steps[i] for i in part]), [whole], *[a[i] for i in part], out,
            scratch=room(n), aliases={n: 0}, specs=([VMEM] * n + [ANY], [ANY]),
        )
    return out.reshape(8 * BLOCK, D), master_out, momentum_out


def solution(mesh):
    parts = Mesh(mesh.devices.reshape(SIZES), AXES)
    rep = ("zhi", "y", "x")
    rows = P(("inner",) + rep, None)
    return jax.shard_map(
        local,
        mesh=parts,
        in_specs=(P(rep, "inner", None), rows, rows),
        out_specs=(P("inner", None), rows, rows),
        check_vma=False,
    )
```

```python
import functools

import jax
import jax.numpy as jnp
from jax import lax
from jax.experimental import pallas as pl
from jax.experimental.pallas import tpu as pltpu
from jax.sharding import Mesh, PartitionSpec as P

N_REP = 32
OUTER_RATE = 0.7
DECAY = 0.9
SCALE = OUTER_RATE * (1 + DECAY)
AXES = ("zhi", "y", "x", "zlo", "core")
SIZES = (2, 4, 4, 4, 2)
D = 2560
HALF = D // 2
ROWS = 20
BLOCK = 80
SMALL = (2 * ROWS, HALF)
FOUR = (4,) + SMALL
F32 = jnp.float32
BF16 = jnp.bfloat16
ANY = pl.BlockSpec(memory_space=pl.ANY)
HBM = pl.BlockSpec(memory_space=pltpu.HBM)
VMEM = pl.BlockSpec(memory_space=pltpu.VMEM)
FIRST = (1, 3, 2)
MIDDLE = (1, 3, 2)
GATHER = (2, 3, 1)
LAST = (2, 3, 1)


def moved(array, axis, place):
    at = AXES.index(axis)
    stride = 1
    for size in SIZES[at + 1:]:
        stride *= size
    pairs = []
    for device in range(256):
        p = device // stride % SIZES[at]
        pairs.append((device, device + (place(p) - p) * stride))
    return lax.ppermute(array, AXES, pairs)


def shifted(array, axis, step):
    return moved(array, axis, lambda p: (p + step) % SIZES[AXES.index(axis)])


def swapped(array, axis, mask):
    return moved(array, axis, lambda p: p ^ mask)


def received(parts, axis, order):
    return [parts[0]] + [shifted(parts[s], axis, s) for s in order]


def call(body, outs, *args, scratch=(), aliases=None, specs=None, after=()):
    size = sum(a.size * a.dtype.itemsize for a in (*args, *outs))
    in_specs, out_specs = specs or ([VMEM] * len(args), [VMEM] * len(outs))
    count = len(args)
    args = (*args, *after)

    def kernel(*refs):
        body(*refs[:count], *refs[len(args):])

    return pl.pallas_call(
        kernel,
        out_shape=outs,
        in_specs=in_specs + [ANY] * len(after),
        out_specs=out_specs,
        scratch_shapes=scratch,
        input_output_aliases=aliases or {},
        cost_estimate=pl.CostEstimate(flops=size, bytes_accessed=size, transcendentals=0),
        compiler_params=pltpu.CompilerParams(vmem_limit_bytes=40 * 2**20),
    )(*args)


def like(shape, dtype):
    return jax.ShapeDtypeStruct(shape, dtype)


def pack_rows(d_ref, *out):
    x = lax.axis_index("x")
    for s in range(4):
        for j in range(4):
            @pl.when(lax.rem(x + s, 4) == j)
            def _():
                for k in range(4):
                    out[s][pl.ds(ROWS * k, ROWS), :] = d_ref[k, pl.ds(ROWS * j, ROWS), :]


def first_sum(axis, *refs):
    parts, out, total = refs[:4], refs[4:8], refs[8]
    place = lax.axis_index(axis)
    for k in range(4):
        rows = pl.ds(ROWS * k, ROWS)
        value = parts[0][rows, :].astype(F32)
        for s in range(1, 4):
            value = value + parts[s][rows, :].astype(F32)
        total[k] = value
    for s in range(4):
        value = total[lax.rem(place + s, 4)]
        o = out[s]
        for col in range(2):
            o[pl.ds(ROWS * col, ROWS), :] = value[:, HALF * col:HALF * (col + 1)].astype(o.dtype)


def second_sum(*refs):
    value = refs[0][...]
    for part in refs[1:4]:
        value = value + part[...].astype(F32)
    refs[4][...] = value.astype(BF16)


def early_base(master, momentum, base):
    base[...] = master[...] - (OUTER_RATE * DECAY * DECAY) * momentum[...]


def new_rows(owner, own, other, base_own, base_other, weights):
    mine = lax.axis_index("zhi") == owner
    for col in range(2):
        rows, cols = pl.ds(ROWS * col, ROWS), pl.ds(HALF * col, HALF)
        average = (own[rows, :].astype(F32) + other[rows, :].astype(F32)) * (1.0 / N_REP)
        base = jnp.where(mine, base_own[:, cols], base_other[:, cols])
        weights[rows, :] = (base - SCALE * average).astype(BF16)


def new_state(own_a, other_a, own_b, other_b, base, momentum, master_out, momentum_out):
    first = lax.axis_index("zhi") == 1
    for col in range(2):
        rows, cols = pl.ds(ROWS * col, ROWS), pl.ds(HALF * col, HALF)
        own = jnp.where(first, own_a[rows, :].astype(F32), own_b[rows, :].astype(F32))
        other = jnp.where(first, other_a[rows, :].astype(F32), other_b[rows, :].astype(F32))
        average = (own + other) * (1.0 / N_REP)
        momentum_out[:, cols] = DECAY * momentum[:, cols] + average
        master_out[:, cols] = base[:, cols] - SCALE * average


def marked(out):
    out[...] = jnp.zeros_like(out)


def join(*refs):
    for h in range(2):
        for part, s in enumerate((0,) + GATHER):
            refs[8 + h][s] = refs[4 * h + part][...]


def unpack_rows(*refs):
    parts, out, block, sems = refs[:4], refs[4], refs[5], refs[6]
    x, y = lax.axis_index("x"), lax.axis_index("y")
    copies = []
    for i in range(4):
        for part, t in enumerate((0,) + LAST):
            for j in range(4):
                @pl.when(lax.rem(x + 4 - t, 4) == j)
                def _():
                    for col in range(2):
                        block[i, pl.ds(ROWS * j, ROWS), pl.ds(HALF * col, HALF)] = parts[part][i, pl.ds(ROWS * col, ROWS), :]
        copies.append(pltpu.make_async_copy(block.at[i], out.at[lax.rem(y + 4 - i, 4)], sems.at[i]))
        copies[-1].start()
    for copy in copies:
        copy.wait()


def unpack_blocks(steps, *refs):
    count = len(steps)
    parts, out, block, sems = refs[:count], refs[count + 1], refs[count + 2], refs[count + 3]
    x, y = lax.axis_index("x"), lax.axis_index("y")
    copies = []
    for part, t in enumerate(steps):
        for i in range(4):
            for j in range(4):
                @pl.when(lax.rem(x + 4 - i, 4) == j)
                def _():
                    for col in range(2):
                        block[part, pl.ds(ROWS * j, ROWS), pl.ds(HALF * col, HALF)] = parts[part][i, pl.ds(ROWS * col, ROWS), :]
        copies.append(pltpu.make_async_copy(block.at[part], out.at[4 + lax.rem(y + 4 - t, 4)], sems.at[part]))
        copies[-1].start()
    for copy in copies:
        copy.wait()


def local(deltas, master, momentum):
    d = deltas.reshape(8, BLOCK, D)
    big = like((BLOCK, D), BF16)
    y = lax.axis_index("y")
    a = [lax.dynamic_index_in_dim(d, 4 + (y + s) % 4, keepdims=False) for s in range(4)]
    b = call(pack_rows, [big] * 4, d[:4])
    a = received(a, "y", FIRST)
    b = received(b, "x", FIRST)
    (base,) = call(early_base, [like((ROWS, D), F32)], master, momentum, after=[a[1]])
    base_other = swapped(base, "zhi", 1)

    outs = [like(SMALL, F32)] + [like(SMALL, BF16)] * 3
    total = [pltpu.VMEM((4, ROWS, D), F32)]
    sum_a = call(functools.partial(first_sum, "x"), outs, *a, scratch=total)
    sum_b = call(functools.partial(first_sum, "y"), outs, *b, scratch=total, after=[sum_a[0]])
    outs = [like(SMALL, BF16)]
    (own_a,) = call(second_sum, outs, *received(sum_a, "x", MIDDLE), after=[sum_b[0], base_other])
    (own_b,) = call(second_sum, outs, *received(sum_b, "y", MIDDLE), after=[own_a])
    other_a = swapped(own_a, "zhi", 1)
    other_b = swapped(own_b, "zhi", 1)
    (new_a,) = call(
        functools.partial(new_rows, 1), outs, own_a, other_a, base, base_other, after=[own_b],
    )
    (new_b,) = call(
        functools.partial(new_rows, 0), outs, own_b, other_b, base, base_other, after=[new_a],
    )
    a, b = received([new_a] * 4, "x", GATHER), received([new_b] * 4, "y", GATHER)
    (mark,) = call(marked, [like((8, 128), F32)], after=a[1:])
    all_a, all_b = call(join, [like(FOUR, BF16)] * 2, *a, *b, after=[swapped(mark, "core", 1)])
    master_out, momentum_out = call(
        new_state, [like((ROWS, D), F32)] * 2, own_a, other_a, own_b, other_b, base, momentum, after=[all_b],
    )
    a = received([all_a] * 4, "y", LAST)
    b = received([all_b] * 4, "x", LAST)
    whole = like((8, BLOCK, D), BF16)
    steps = (0,) + LAST

    def room(count):
        return [pltpu.VMEM((count, BLOCK, D), BF16), pltpu.SemaphoreType.DMA((count,))]

    (out,) = call(unpack_rows, [whole], *b, scratch=room(4), specs=([VMEM] * 4, [ANY]))
    for part in ((0, 1, 2), (3,)):
        n = len(part)
        (out,) = call(
            functools.partial(unpack_blocks, [steps[i] for i in part]), [whole], *[a[i] for i in part], out,
            scratch=room(n), aliases={n: 0}, specs=([VMEM] * n + [ANY], [ANY]),
        )
    return out.reshape(8 * BLOCK, D), master_out, momentum_out


def solution(mesh):
    parts = Mesh(mesh.devices.reshape(SIZES), AXES)
    rep, inner = ("zhi", "y", "x"), ("zlo", "core")
    rows = P(inner + rep, None)
    return jax.shard_map(
        local,
        mesh=parts,
        in_specs=(P(rep, inner, None), rows, rows),
        out_specs=(P(inner, None), rows, rows),
        check_vma=False,
    )
```

```python
import functools

import jax
import jax.numpy as jnp
from jax import lax
from jax.experimental import pallas as pl
from jax.experimental.pallas import tpu as pltpu
from jax.sharding import Mesh, PartitionSpec as P

N_REP = 32
OUTER_RATE = 0.7
DECAY = 0.9
SCALE = OUTER_RATE * (1 + DECAY)
AXES = ("zhi", "y", "x", "zlo", "core")
SIZES = (2, 4, 4, 4, 2)
D = 2560
HALF = D // 2
ROWS = 20
BLOCK = 80
SMALL = (2 * ROWS, HALF)
FOUR = (4,) + SMALL
F32 = jnp.float32
BF16 = jnp.bfloat16
ANY = pl.BlockSpec(memory_space=pl.ANY)
HBM = pl.BlockSpec(memory_space=pltpu.HBM)
VMEM = pl.BlockSpec(memory_space=pltpu.VMEM)
FIRST = (1, 3, 2)
MIDDLE = (1, 3, 2)
GATHER = (2, 3, 1)
LAST = (2, 3, 1)


def moved(array, axis, place):
    at = AXES.index(axis)
    stride = 1
    for size in SIZES[at + 1:]:
        stride *= size
    pairs = []
    for device in range(256):
        p = device // stride % SIZES[at]
        pairs.append((device, device + (place(p) - p) * stride))
    return lax.ppermute(array, AXES, pairs)


def shifted(array, axis, step):
    return moved(array, axis, lambda p: (p + step) % SIZES[AXES.index(axis)])


def swapped(array, axis, mask):
    return moved(array, axis, lambda p: p ^ mask)


def received(parts, axis, order):
    return [parts[0]] + [shifted(parts[s], axis, s) for s in order]


def call(body, outs, *args, scratch=(), aliases=None, specs=None, after=()):
    size = sum(a.size * a.dtype.itemsize for a in (*args, *outs))
    in_specs, out_specs = specs or ([VMEM] * len(args), [VMEM] * len(outs))
    count = len(args)
    args = (*args, *after)

    def kernel(*refs):
        body(*refs[:count], *refs[len(args):])

    return pl.pallas_call(
        kernel,
        out_shape=outs,
        in_specs=in_specs + [ANY] * len(after),
        out_specs=out_specs,
        scratch_shapes=scratch,
        input_output_aliases=aliases or {},
        cost_estimate=pl.CostEstimate(flops=size, bytes_accessed=size, transcendentals=0),
        compiler_params=pltpu.CompilerParams(vmem_limit_bytes=40 * 2**20),
    )(*args)


def like(shape, dtype):
    return jax.ShapeDtypeStruct(shape, dtype)


def pack_rows(d_ref, *out):
    x = lax.axis_index("x")
    for s in range(4):
        for j in range(4):
            @pl.when(lax.rem(x + s, 4) == j)
            def _():
                for k in range(4):
                    out[s][pl.ds(ROWS * k, ROWS), :] = d_ref[k, pl.ds(ROWS * j, ROWS), :]


def first_sum(axis, *refs):
    parts, out, total = refs[:4], refs[4:8], refs[8]
    place = lax.axis_index(axis)
    for k in range(4):
        rows = pl.ds(ROWS * k, ROWS)
        value = parts[0][rows, :].astype(F32)
        for s in range(1, 4):
            value = value + parts[s][rows, :].astype(F32)
        total[k] = value
    for s in range(4):
        value = total[lax.rem(place + s, 4)]
        o = out[s]
        for col in range(2):
            o[pl.ds(ROWS * col, ROWS), :] = value[:, HALF * col:HALF * (col + 1)].astype(o.dtype)


def second_sum(*refs):
    value = refs[0][...]
    for part in refs[1:4]:
        value = value + part[...].astype(F32)
    refs[4][...] = value.astype(BF16)


def early_base(master, momentum, base):
    base[...] = master[...] - (OUTER_RATE * DECAY * DECAY) * momentum[...]


def new_rows(owner, own, other, base_own, base_other, weights):
    mine = lax.axis_index("zhi") == owner
    for col in range(2):
        rows, cols = pl.ds(ROWS * col, ROWS), pl.ds(HALF * col, HALF)
        average = (own[rows, :].astype(F32) + other[rows, :].astype(F32)) * (1.0 / N_REP)
        base = jnp.where(mine, base_own[:, cols], base_other[:, cols])
        weights[rows, :] = (base - SCALE * average).astype(BF16)


def new_state(own_a, other_a, own_b, other_b, base, momentum, master_out, momentum_out):
    first = lax.axis_index("zhi") == 1
    for col in range(2):
        rows, cols = pl.ds(ROWS * col, ROWS), pl.ds(HALF * col, HALF)
        own = jnp.where(first, own_a[rows, :].astype(F32), own_b[rows, :].astype(F32))
        other = jnp.where(first, other_a[rows, :].astype(F32), other_b[rows, :].astype(F32))
        average = (own + other) * (1.0 / N_REP)
        momentum_out[:, cols] = DECAY * momentum[:, cols] + average
        master_out[:, cols] = base[:, cols] - SCALE * average


def marked(out):
    out[...] = jnp.zeros_like(out)


def join(*refs):
    for h in range(2):
        for part, s in enumerate((0,) + GATHER):
            refs[8 + h][s] = refs[4 * h + part][...]


def unpack_rows(*refs):
    parts, out, block, sems = refs[:4], refs[4], refs[5], refs[6]
    x, y = lax.axis_index("x"), lax.axis_index("y")
    copies = []
    for i in range(4):
        for part, t in enumerate((0,) + LAST):
            for j in range(4):
                @pl.when(lax.rem(x + 4 - t, 4) == j)
                def _():
                    for col in range(2):
                        block[i, pl.ds(ROWS * j, ROWS), pl.ds(HALF * col, HALF)] = parts[part][i, pl.ds(ROWS * col, ROWS), :]
        copies.append(pltpu.make_async_copy(block.at[i], out.at[lax.rem(y + 4 - i, 4)], sems.at[i]))
        copies[-1].start()
    for copy in copies:
        copy.wait()


def unpack_blocks(steps, *refs):
    count = len(steps)
    parts, out, block, sems = refs[:count], refs[count + 1], refs[count + 2], refs[count + 3]
    x, y = lax.axis_index("x"), lax.axis_index("y")
    copies = []
    for part, t in enumerate(steps):
        for i in range(4):
            for j in range(4):
                @pl.when(lax.rem(x + 4 - i, 4) == j)
                def _():
                    for col in range(2):
                        block[part, pl.ds(ROWS * j, ROWS), pl.ds(HALF * col, HALF)] = parts[part][i, pl.ds(ROWS * col, ROWS), :]
        copies.append(pltpu.make_async_copy(block.at[part], out.at[4 + lax.rem(y + 4 - t, 4)], sems.at[part]))
        copies[-1].start()
    for copy in copies:
        copy.wait()


def local(deltas, master, momentum):
    d = deltas.reshape(8, BLOCK, D)
    big = like((BLOCK, D), BF16)
    y = lax.axis_index("y")
    a = [lax.dynamic_index_in_dim(d, 4 + (y + s) % 4, keepdims=False) for s in range(4)]
    b = call(pack_rows, [big] * 4, d[:4])
    a = received(a, "y", FIRST)
    b = received(b, "x", LAST)
    (base,) = call(early_base, [like((ROWS, D), F32)], master, momentum, after=[a[1]])
    base_other = swapped(base, "zhi", 1)

    outs = [like(SMALL, F32)] + [like(SMALL, BF16)] * 3
    total = [pltpu.VMEM((4, ROWS, D), F32)]
    sum_a = call(functools.partial(first_sum, "x"), outs, *a, scratch=total)
    sum_b = call(functools.partial(first_sum, "y"), outs, *b, scratch=total, after=[sum_a[0]])
    outs = [like(SMALL, BF16)]
    (own_a,) = call(second_sum, outs, *received(sum_a, "x", MIDDLE), after=[sum_b[0], base_other])
    (own_b,) = call(second_sum, outs, *received(sum_b, "y", MIDDLE), after=[own_a])
    other_a = swapped(own_a, "zhi", 1)
    other_b = swapped(own_b, "zhi", 1)
    (new_a,) = call(
        functools.partial(new_rows, 1), outs, own_a, other_a, base, base_other, after=[own_b],
    )
    (new_b,) = call(
        functools.partial(new_rows, 0), outs, own_b, other_b, base, base_other, after=[new_a],
    )
    a, b = received([new_a] * 4, "x", GATHER), received([new_b] * 4, "y", GATHER)
    (mark,) = call(marked, [like((8, 128), F32)], after=a[1:])
    all_a, all_b = call(join, [like(FOUR, BF16)] * 2, *a, *b, after=[swapped(mark, "core", 1)])
    master_out, momentum_out = call(
        new_state, [like((ROWS, D), F32)] * 2, own_a, other_a, own_b, other_b, base, momentum, after=[all_b],
    )
    a = received([all_a] * 4, "y", LAST)
    b = received([all_b] * 4, "x", LAST)
    whole = like((8, BLOCK, D), BF16)
    steps = (0,) + LAST

    def room(count):
        return [pltpu.VMEM((count, BLOCK, D), BF16), pltpu.SemaphoreType.DMA((count,))]

    (out,) = call(unpack_rows, [whole], *b, scratch=room(4), specs=([VMEM] * 4, [ANY]))
    for part in ((0, 1, 2), (3,)):
        n = len(part)
        (out,) = call(
            functools.partial(unpack_blocks, [steps[i] for i in part]), [whole], *[a[i] for i in part], out,
            scratch=room(n), aliases={n: 0}, specs=([VMEM] * n + [ANY], [ANY]),
        )
    return out.reshape(8 * BLOCK, D), master_out, momentum_out


def solution(mesh):
    parts = Mesh(mesh.devices.reshape(SIZES), AXES)
    rep, inner = ("zhi", "y", "x"), ("zlo", "core")
    rows = P(inner + rep, None)
    return jax.shard_map(
        local,
        mesh=parts,
        in_specs=(P(rep, inner, None), rows, rows),
        out_specs=(P(inner, None), rows, rows),
        check_vma=False,
    )
```
